32 devices in a mesh: slab: 4 (over y, core), dp: 8 (over z, x).
Axes of the slice: x: 2, y: 2, z: 4, core: 2. Of those that a mesh axis runs over, the one named last changes fastest.
Arguments:
- inputs: bfloat16 [8, 32, 24, 64, 128], P('dp', 'slab'), may hold values from -6 to 6
- cotangent: bfloat16 [8, 32, 24, 64, 128], P('dp', 'slab'), may hold values from -4 to 4
- spectral_weight: bfloat16 [16, 256, 4096], P('slab', 'dp'), may hold values from -1.5 to 1.5
- w_in: bfloat16 [64, 256], replicated, may hold values from -0.75 to 0.75
- b_in: float32 [256], replicated, may hold values from -3 to 3
- w_out: bfloat16 [256, 64], replicated, may hold values from -0.375 to 0.375
- b_out: float32 [64], replicated, may hold values from -3 to 3
Outputs:
- grad_inputs: bfloat16 [8, 32, 24, 64, 128], P('dp', 'slab')
- grad_spectral: float32 [16, 256, 4096], P('slab', 'dp')
The draws below stay inside these ranges and needn't reach their ends.
All inputs are finite; a program needn't handle non-finite values.
Results may differ from the reference program's by a relative error of at most 0.014.
Values may be sent and summed in bfloat16 or wider, within the bound.
A program may use at most 128 MiB of HBM per device.

```python
import math
import jax
import jax.numpy as jnp
from jax import lax

C = 64
H = 256
MX = 16
MY = 16
MZ = 16
NX = 32
NY = 24
NZ = 128
BATCH = 8


def shard_levels(stream_key, shape, shards, smallest, top_value):
    level, own = 1.0, jax.random.fold_in(stream_key, 6)
    for dim, blocks in shards:
        steps = jnp.exp(jax.random.uniform(jax.random.fold_in(own, dim), (blocks,), jnp.float32, smallest / len(shards), top_value / len(shards)))
        level = level * jnp.repeat(steps, shape[dim] // blocks).reshape([-1 if axis == dim else 1 for axis in range(len(shape))])
    return level


def gaussian(stream_key, shape, deviation, reach, pieces=(), held_as=jnp.bfloat16):
    drawn = jax.random.normal(stream_key, shape, jnp.float32) * deviation
    if len(pieces) > 0:
        drawn = shard_levels(stream_key, shape, pieces, -0.22, 0.18) * drawn
    return jnp.clip(drawn, min=-reach, max=reach).astype(held_as)


def setup_inputs(seed: int = 0) -> dict:
    splits = jax.random.split(jax.random.key(seed), 8)
    inputs = gaussian(splits[0], (BATCH, NX, NY, C, NZ), 1.0, 6.0, ((0, 8), (1, 4)))
    cotangent = gaussian(splits[1], (BATCH, NX, NY, C, NZ), 0.5, 4.0, ((0, 8), (1, 4)))
    spectral_weight = gaussian(splits[2], (MY, MX * MZ, C * C), (C // 4) ** -0.5, 1.5, ((0, 4), (1, 8)))
    w_in = gaussian(splits[3], (C, H), C ** -0.5, 0.75)
    b_in = gaussian(splits[4], (H,), 0.5, 3.0, (), jnp.float32)
    w_out = gaussian(splits[5], (H, C), H ** -0.5, 0.375)
    b_out = gaussian(splits[6], (C,), 0.5, 3.0, (), jnp.float32)
    return {"inputs": inputs, "cotangent": cotangent, "spectral_weight": spectral_weight, "w_in": w_in, "b_in": b_in, "w_out": w_out, "b_out": b_out}


root_half = 0.7071067811865476
inv_root_two_pi = 0.3989422804014327


def dft_table(length, kept_count):
    half_kept = kept_count // 2
    positions = jnp.arange(length, dtype=jnp.int32)
    cos_freq = jnp.arange(half_kept, dtype=jnp.int32)
    freqs = jnp.concatenate([cos_freq, cos_freq + 1])[:, None]
    phases = ((freqs * positions[None, :]) % length).astype(jnp.float32) * (2.0 * math.pi / length)
    values = jnp.concatenate([jnp.cos(phases[:half_kept]), jnp.sin(phases[half_kept:])], axis=0)
    return values.astype(jnp.bfloat16)


def gelu_value(values_in):
    return 0.5 * values_in * (1.0 + jax.scipy.special.erf(values_in * root_half))


def gelu_slope(values_in):
    return 0.5 * (1.0 + jax.scipy.special.erf(values_in * root_half)) + values_in * jnp.exp(-0.5 * values_in * values_in) * inv_root_two_pi


def fdot(form, left, right):
    return jnp.einsum(form, left.astype(jnp.float32), right.astype(jnp.float32))


def reference(inputs, cotangent, spectral_weight, w_in, b_in, w_out, b_out):
    table_x = dft_table(NX, MX)
    table_y = dft_table(NY, MY)
    table_z = dft_table(NZ, MZ)
    factor = 8.0 / (NX * NY * NZ)
    weights = spectral_weight.reshape(MY, MX, MZ, C, C)

    def analyse(samples):
        along_z = fdot('xycz,kz->xyck', samples, table_z).astype(jnp.bfloat16)
        along_y = fdot('xyck,jy->xjck', along_z, table_y).astype(jnp.bfloat16)
        return fdot('xjck,ix->ijck', along_y, table_x).astype(jnp.bfloat16)

    def synthesise(coeff_in):
        back_x = fdot('ijck,ix->xjck', coeff_in, table_x).astype(jnp.bfloat16)
        back_y = fdot('xjck,jy->xyck', back_x, table_y).astype(jnp.bfloat16)
        return fdot('xyck,kz->xycz', back_y, table_z) * factor

    def one_crop(running, crop_pair):
        samples, upstream = crop_pair
        coeffs = analyse(samples)
        mixed_modes = fdot('ijck,jikco->ijok', coeffs, weights).astype(jnp.bfloat16)
        spectral = synthesise(mixed_modes)
        activation = fdot('xycz,ch->xyhz', samples, w_in) + b_in.astype(jnp.float32)[:, None]
        hidden = gelu_value(activation).astype(jnp.bfloat16)
        pre_gelu = fdot('xyhz,hc->xycz', hidden, w_out) + b_out.astype(jnp.float32)[:, None] + spectral
        grad_pre = (upstream.astype(jnp.float32) * gelu_slope(pre_gelu)).astype(jnp.bfloat16)
        grad_act = (fdot('xycz,hc->xyhz', grad_pre, w_out) * gelu_slope(activation)).astype(jnp.bfloat16)
        grad_coeffs = analyse(grad_pre)
        back_modes = fdot('ijok,jikco->ijck', grad_coeffs, weights).astype(jnp.bfloat16)
        grad_field = (fdot('xyhz,ch->xycz', grad_act, w_in) + synthesise(back_modes)).astype(jnp.bfloat16)
        grad_term = fdot('ijck,ijok->jikco', coeffs, grad_coeffs) * factor
        return running + grad_term, grad_field

    start_sum = jnp.zeros((MY, MX, MZ, C, C), jnp.float32)
    running, grad_inputs = lax.scan(one_crop, start_sum, (inputs, cotangent))
    return grad_inputs, running.reshape(MY, MX * MZ, C * C)
```

```python
import functools
import math

import jax
import jax.numpy as jnp
import ml_dtypes
import numpy as np
from jax import lax
from jax.experimental import pallas as pl
from jax.experimental.pallas import tpu as pltpu
from jax.sharding import PartitionSpec as P

C = 64
MX = 16
MY = 16
MZ = 16
NX = 32
NY = 24
NZ = 128


root_half = 0.7071067811865476
inv_root_two_pi = 0.3989422804014327


def dft_table(length, kept_count):
    half_kept = kept_count // 2
    positions = jnp.arange(length, dtype=jnp.int32)
    cos_freq = jnp.arange(half_kept, dtype=jnp.int32)
    freqs = jnp.concatenate([cos_freq, cos_freq + 1])[:, None]
    phases = (freqs * positions[None, :] % length).astype(jnp.float32) * (2.0 * math.pi / length)
    values = jnp.concatenate([jnp.cos(phases[:half_kept]), jnp.sin(phases[half_kept:])], axis=0)
    return values.astype(jnp.bfloat16)


def gelu_value(values_in):
    return 0.5 * values_in * (1.0 + jax.scipy.special.erf(values_in * root_half))


def gelu_slope(values_in):
    return (
        0.5 * (1.0 + jax.scipy.special.erf(values_in * root_half))
        + values_in * jnp.exp(-0.5 * values_in * values_in) * inv_root_two_pi
    )


def bdot(form, left, right):
    return jnp.einsum(form, left, right, preferred_element_type=jnp.float32)


def per_device(inputs, cotangent, spectral_weight, w_in, b_in, w_out, b_out):
    slab_count = lax.axis_size("slab")
    group_count = lax.axis_size("dp")
    local_modes = MY // slab_count
    group_modes = MX * MZ // group_count
    crop_count = inputs.shape[0]
    table_x = dft_table(NX, MX)
    table_y = dft_table(NY, MY)
    table_z = dft_table(NZ, MZ)
    factor = 8.0 / (NX * NY * NZ)

    def analyse(samples):
        along_z = bdot("bxycz,kz->bxyck", samples, table_z).astype(jnp.bfloat16)
        along_y = bdot("bxyck,jy->bxjck", along_z, table_y).astype(jnp.bfloat16)
        return bdot(
            "bxjck,ix->bijck",
            lax.all_to_all(along_y, "slab", split_axis=2, concat_axis=1, tiled=True),
            table_x,
        ).astype(jnp.bfloat16)

    def synthesise(coeff_in):
        back_x = bdot("bijck,ix->bxjck", coeff_in, table_x).astype(jnp.bfloat16)
        back_y = bdot(
            "bxjck,jy->bxyck",
            lax.all_to_all(back_x, "slab", split_axis=1, concat_axis=2, tiled=True),
            table_y,
        ).astype(jnp.bfloat16)
        return bdot("bxyck,kz->bxycz", back_y, table_z) * factor

    def send_out(coeff_in):
        ordered = jnp.transpose(coeff_in, (0, 2, 1, 4, 3)).reshape(
            crop_count, local_modes, group_count, group_modes, C
        )
        arrived = lax.all_to_all(ordered, "dp", split_axis=2, concat_axis=0, tiled=True)
        return arrived.reshape(crop_count * group_count, local_modes, group_modes, C)

    def send_back(mixed_in):
        shaped = mixed_in.reshape(crop_count * group_count, local_modes, 1, group_modes, C)
        arrived = lax.all_to_all(shaped, "dp", split_axis=0, concat_axis=2, tiled=True)
        return jnp.transpose(arrived.reshape(crop_count, local_modes, MX, MZ, C), (0, 2, 1, 4, 3))

    owned = spectral_weight.reshape(local_modes, group_modes, C, C)
    coeffs = analyse(inputs)
    routed = send_out(coeffs)
    mixed_modes = send_back(bdot("bjgc,jgco->bjgo", routed, owned).astype(jnp.bfloat16))
    spectral = synthesise(mixed_modes)
    activation = bdot("bxycz,ch->bxyhz", inputs, w_in) + b_in[:, None]
    hidden = gelu_value(activation).astype(jnp.bfloat16)
    pre_gelu = bdot("bxyhz,hc->bxycz", hidden, w_out) + b_out[:, None] + spectral
    grad_pre = (cotangent.astype(jnp.float32) * gelu_slope(pre_gelu)).astype(jnp.bfloat16)
    grad_act = (bdot("bxycz,hc->bxyhz", grad_pre, w_out) * gelu_slope(activation)).astype(
        jnp.bfloat16
    )
    grad_coeffs = analyse(grad_pre)
    grad_routed = send_out(grad_coeffs)
    back_modes = send_back(bdot("bjgo,jgco->bjgc", grad_routed, owned).astype(jnp.bfloat16))
    grad_weight = (bdot("bjgc,bjgo->jgco", routed, grad_routed) * factor).reshape(
        local_modes, group_modes, C * C
    )
    grad_field = (bdot("bxyhz,ch->bxycz", grad_act, w_in) + synthesise(back_modes)).astype(
        jnp.bfloat16
    )
    return (grad_field, grad_weight)


SLABS = 4
GROUPS = 8
XL = NX // SLABS
JL = MY // SLABS
GM = MX * MZ // GROUPS
HID = 256
UNITS = XL * NY // 4
FACTOR = 8.0 / (NX * NY * NZ)
F32 = jnp.float32
BF16 = jnp.bfloat16
STEP = 512


def host_table(length, kept):
    freq = np.concatenate([np.arange(kept // 2), np.arange(kept // 2) + 1])[:, None]
    phase = (freq * np.arange(length)[None, :] % length).astype(np.float32)
    phase = phase * np.float32(2.0 * math.pi / length)
    return np.concatenate([np.cos(phase[: kept // 2]), np.sin(phase[kept // 2 :])], axis=0)


def host_tables():
    eye = np.eye(MZ, dtype=np.float32)
    kz = np.kron(np.eye(8, dtype=np.float32), host_table(NZ, MZ))
    ky = np.kron(host_table(NY, MY), eye)
    kx = np.kron(host_table(NX, MX), eye)
    spread = np.repeat(np.eye(C, dtype=np.float32), C, axis=1)
    tables = (kz, kz.T, ky, ky.T, kx, kx.T, spread, spread.T)
    return tuple(jnp.asarray(np.ascontiguousarray(t).astype(ml_dtypes.bfloat16)) for t in tables)


def dot(left, right):
    return jnp.dot(left, right, preferred_element_type=F32)


def fused_kernel(
    x_hbm, ct_hbm, w_hbm, w_in, w_in_t, b_in, w_out, w_out_t, b_out,
    kz, kz_t, ky, ky_t, kx, kx_t, spread, spread_t,
    gx_hbm, gw_hbm,
    x_v, ct_v, w_v, gw_v, slope_v, part_v, gp_v, along_z, rows_v,
    send_s, recv_s, send_g, recv_g, send_sem, recv_sem, load_sem, store_sem,
):
    slab = lax.axis_index("slab")
    group = lax.axis_index("dp")

    loads = [
        pltpu.make_async_copy(x_hbm, x_v, load_sem.at[0]),
        pltpu.make_async_copy(ct_hbm, ct_v, load_sem.at[1]),
        pltpu.make_async_copy(w_hbm, w_v, load_sem.at[2]),
    ]
    for load in loads:
        load.start()

    barrier = pltpu.get_barrier_semaphore()
    for r in range(1, SLABS):
        pl.semaphore_signal(
            barrier, inc=1, device_id={"slab": lax.rem(slab + r, SLABS)},
            device_id_type=pl.DeviceIdType.MESH,
        )
    for r in range(1, GROUPS):
        pl.semaphore_signal(
            barrier, inc=1, device_id={"dp": lax.rem(group + r, GROUPS)},
            device_id_type=pl.DeviceIdType.MESH,
        )

    def exchange(phase, send, recv, axis, me, count):
        copies = []
        for r in range(1, count):
            dest = lax.rem(me + r, count)
            copy = pltpu.make_async_remote_copy(
                src_ref=send.at[dest],
                dst_ref=recv.at[me],
                send_sem=send_sem.at[phase, r - 1],
                recv_sem=recv_sem.at[phase, r - 1],
                device_id={axis: dest},
                device_id_type=pl.DeviceIdType.MESH,
            )
            copy.start()
            copies.append(copy)
        recv[me] = send[me]
        return copies

    def finish(copies):
        for copy in copies:
            copy.wait()

    def over_slabs(phase):
        return exchange(phase, send_s.at[phase // 2], recv_s.at[phase // 2], "slab", slab, SLABS)

    def over_groups(phase):
        return exchange(phase, send_g.at[phase // 2], recv_g.at[phase // 2], "dp", group, GROUPS)

    def lanes_of(ref, plane, first, count):
        return jnp.concatenate([ref[plane * NY + first + q] for q in range(count)], axis=1)

    def send_along_y(phase):
        along_y = dot(along_z[...], ky_t[...])
        for xl in range(XL):
            turned = along_y[xl * C : (xl + 1) * C].T
            for s in range(SLABS):
                for p in range(JL // 2):
                    j = s * JL + 2 * p
                    pair = jnp.concatenate(
                        [turned[j * MZ : (j + 1) * MZ], turned[(j + 1) * MZ : (j + 2) * MZ]], axis=1
                    )
                    send_s[phase // 2, s, xl * MZ : (xl + 1) * MZ, 2 * p * C : 2 * (p + 1) * C] = (
                        pair.astype(BF16)
                    )
        return over_slabs(phase)

    def send_modes(phase):
        arrived = recv_s[(phase - 1) // 2].reshape(NX * MZ, JL * C)
        modes = dot(kx[...], arrived).astype(BF16)
        send_g[phase // 2] = modes.reshape(GROUPS, GM, JL * C)
        return over_groups(phase)

    def send_planes(phase):
        arrived = recv_g[(phase - 1) // 2].reshape(MX * MZ, JL * C)
        planes = dot(kx_t[...], arrived).astype(BF16)
        send_s[phase // 2] = planes.reshape(SLABS, XL * MZ, JL * C)
        return over_slabs(phase)

    def back_along_y(phase):
        for xl in range(XL):
            blocks = []
            for s in range(SLABS):
                rows = recv_s[phase // 2, s, xl * MZ : (xl + 1) * MZ, :].astype(F32)
                for jl in range(JL):
                    blocks.append(rows[:, jl * C : (jl + 1) * C])
            turned = jnp.concatenate(blocks, axis=0).T
            rows_v[xl * C : (xl + 1) * C, :] = turned.astype(BF16)
        along_z[...] = dot(rows_v[...], ky[...]).astype(BF16)

    def plane_rows(xl):
        return pl.ds(pl.multiple_of(xl * C, C), C)

    def forward_units(first, last):
        def unit(u, carry):
            plane, part = u // (NY // 4), lax.rem(u, NY // 4)
            samples = lanes_of(x_v, plane, part * 4, 4)
            act = dot(w_in_t[...], samples) + b_in[...]
            phi = 0.5 + 0.5 * lax.erf(act * root_half)
            bell = jnp.exp(act * act * -0.5) * inv_root_two_pi
            slope_v[u] = (phi + act * bell).astype(BF16)
            part_v[u] = dot(w_out_t[...], (act * phi).astype(BF16)) + b_out[...]
            return carry

        lax.fori_loop(first, last, unit, 0)

    def backward_units(first, last):
        def unit(u, carry):
            grad = dot(w_out[...], gp_v[u]) * slope_v[u].astype(F32)
            part_v[u] = dot(w_in[...], grad.astype(BF16))
            return carry

        lax.fori_loop(first, last, unit, 0)

    loads[0].wait()

    def analyse_plane(xl, carry):
        for t in range(NY // 8):
            samples = lanes_of(x_v, xl, t * 8, 8)
            along_z[plane_rows(xl), t * 128 : (t + 1) * 128] = dot(samples, kz_t[...]).astype(BF16)
        return carry

    lax.fori_loop(0, XL, analyse_plane, 0)
    pl.semaphore_wait(barrier, SLABS + GROUPS - 2)
    flight = send_along_y(0)
    forward_units(0, 12)
    finish(flight)
    flight = send_modes(1)
    forward_units(12, 24)
    finish(flight)

    loads[2].wait()
    coeffs = recv_g.at[0]
    grads = recv_g.at[2]

    def pair_rows(ref, p):
        return ref[:, :, 2 * p * C : 2 * (p + 1) * C].reshape(GROUPS * GM, 2 * C)

    for p in range(JL // 2):
        pair = pair_rows(coeffs, p)
        mixed = []
        for half in range(2):
            jl = 2 * p + half
            rows = pair[:, half * C : (half + 1) * C]

            def mix(n, total, rows=rows, jl=jl):
                span = pl.ds(pl.multiple_of(n * STEP, STEP), STEP)
                wide = dot(rows, spread[:, span]).reshape(GROUPS, GM, STEP)
                term = (wide * w_v[jl, :, span].astype(F32)[None]).reshape(GROUPS * GM, STEP)
                return total + sum(term[:, q * 128 : (q + 1) * 128] for q in range(STEP // 128))

            total = lax.fori_loop(0, C * C // STEP, mix, jnp.zeros((GROUPS * GM, 2 * C), F32))
            mixed.append(total[:, :C] + total[:, C:])
        send_g[1, :, :, 2 * p * C : 2 * (p + 1) * C] = (
            jnp.concatenate(mixed, axis=1).astype(BF16).reshape(GROUPS, GM, 2 * C)
        )
    flight = over_groups(2)
    forward_units(24, 36)
    finish(flight)
    flight = send_planes(3)
    forward_units(36, UNITS)
    finish(flight)
    back_along_y(3)

    loads[1].wait()

    def middle_plane(xl, carry):
        for t in range(NY // 8):
            kept = along_z[plane_rows(xl), t * 128 : (t + 1) * 128]
            u = xl * (NY // 4) + 2 * t
            pre = jnp.concatenate([part_v[u], part_v[u + 1]], axis=1) + dot(kept, kz[...]) * FACTOR
            phi = 0.5 + 0.5 * lax.erf(pre * root_half)
            slope = phi + pre * jnp.exp(pre * pre * -0.5) * inv_root_two_pi
            grad = (lanes_of(ct_v, xl, t * 8, 8).astype(F32) * slope).astype(BF16)
            gp_v[u] = grad[:, :512]
            gp_v[u + 1] = grad[:, 512:]
            along_z[plane_rows(xl), t * 128 : (t + 1) * 128] = dot(grad, kz_t[...]).astype(BF16)
        return carry

    lax.fori_loop(0, XL, middle_plane, 0)
    flight = send_along_y(4)
    backward_units(0, 16)
    finish(flight)
    flight = send_modes(5)
    backward_units(16, 32)
    finish(flight)

    for p in range(JL // 2):
        pair = pair_rows(grads, p).astype(F32)
        mixed = []
        for half in range(2):
            jl = 2 * p + half
            rows = pair[:, half * C : (half + 1) * C]
            twice = jnp.concatenate([rows, rows], axis=1)
            wide = jnp.concatenate([twice] * (STEP // 128), axis=1).reshape(GROUPS, GM, STEP)

            def mix_back(n, total, wide=wide, jl=jl):
                span = pl.ds(pl.multiple_of(n * STEP, STEP), STEP)
                term = wide * w_v[jl, :, span].astype(F32)[None]
                return total + dot(term.astype(BF16).reshape(GROUPS * GM, STEP), spread_t[span, :])

            mixed.append(
                lax.fori_loop(0, C * C // STEP, mix_back, jnp.zeros((GROUPS * GM, C), F32))
            )
        send_g[3, :, :, 2 * p * C : 2 * (p + 1) * C] = (
            jnp.concatenate(mixed, axis=1).astype(BF16).reshape(GROUPS, GM, 2 * C)
        )
    flight = over_groups(6)

    for p in range(JL // 2):
        pair = pair_rows(coeffs, p)
        grad_pair = pair_rows(grads, p).astype(F32)
        for half in range(2):
            jl = 2 * p + half
            rows = pair[:, half * C : (half + 1) * C]
            grad_rows = grad_pair[:, half * C : (half + 1) * C] * FACTOR
            twice = jnp.concatenate([grad_rows, grad_rows], axis=1)
            wide = jnp.concatenate([twice] * (STEP // 128), axis=1)

            def outer(n, carry, rows=rows, wide=wide, jl=jl):
                span = pl.ds(pl.multiple_of(n * STEP, STEP), STEP)
                term = (dot(rows, spread[:, span]) * wide).reshape(GROUPS, GM, STEP)
                gw_v[jl, :, span] = jnp.sum(term, axis=0)
                return carry

            lax.fori_loop(0, C * C // STEP, outer, 0)
    store_gw = pltpu.make_async_copy(gw_v, gw_hbm, store_sem.at[0])
    store_gw.start()
    finish(flight)
    flight = send_planes(7)
    backward_units(32, UNITS)
    finish(flight)
    back_along_y(7)

    def last_plane(xl, carry):
        for t in range(NY // 8):
            kept = along_z[plane_rows(xl), t * 128 : (t + 1) * 128]
            u = xl * (NY // 4) + 2 * t
            total = jnp.concatenate([part_v[u], part_v[u + 1]], axis=1)
            total = (total + dot(kept, kz[...]) * FACTOR).astype(BF16)
            for q in range(8):
                ct_v[xl * NY + t * 8 + q] = total[:, q * NZ : (q + 1) * NZ]
        return carry

    lax.fori_loop(0, XL, last_plane, 0)
    store_gx = pltpu.make_async_copy(ct_v, gx_hbm, store_sem.at[1])
    store_gx.start()
    store_gw.wait()
    store_gx.wait()


def fused_device(inputs, cotangent, spectral_weight, w_in, b_in, w_out, b_out):
    field = inputs.shape
    flat = (XL * NY, C, NZ)
    any_spec = pl.BlockSpec(memory_space=pl.ANY)
    vmem_spec = pl.BlockSpec(memory_space=pltpu.VMEM)
    out = pl.pallas_call(
        fused_kernel,
        out_shape=(
            jax.ShapeDtypeStruct(flat, BF16),
            jax.ShapeDtypeStruct((JL, GM, C * C), F32),
        ),
        in_specs=[any_spec] * 3 + [vmem_spec] * 14,
        out_specs=(any_spec, any_spec),
        scratch_shapes=[
            pltpu.VMEM(flat, BF16),
            pltpu.VMEM(flat, BF16),
            pltpu.VMEM((JL, GM, C * C), BF16),
            pltpu.VMEM((JL, GM, C * C), F32),
            pltpu.VMEM((UNITS, HID, 4 * NZ), BF16),
            pltpu.VMEM((UNITS, C, 4 * NZ), F32),
            pltpu.VMEM((UNITS, C, 4 * NZ), BF16),
            pltpu.VMEM((XL * C, NY * MZ), BF16),
            pltpu.VMEM((XL * C, MY * MZ), BF16),
            pltpu.VMEM((4, SLABS, XL * MZ, JL * C), BF16),
            pltpu.VMEM((4, SLABS, XL * MZ, JL * C), BF16),
            pltpu.VMEM((4, GROUPS, GM, JL * C), BF16),
            pltpu.VMEM((4, GROUPS, GM, JL * C), BF16),
            pltpu.SemaphoreType.DMA((8, GROUPS - 1)),
            pltpu.SemaphoreType.DMA((8, GROUPS - 1)),
            pltpu.SemaphoreType.DMA((3,)),
            pltpu.SemaphoreType.DMA((2,)),
        ],
        compiler_params=pltpu.CompilerParams(
            collective_id=0, has_side_effects=True, vmem_limit_bytes=60 * 1024 * 1024
        ),
    )(
        inputs.reshape(flat), cotangent.reshape(flat), spectral_weight,
        w_in, w_in.T, b_in[:, None], w_out, w_out.T, b_out[:, None], *host_tables(),
    )
    return out[0].reshape(field), out[1]


def solution(mesh):
    sizes = (mesh.shape["slab"], mesh.shape["dp"])
    body = fused_device if sizes == (SLABS, GROUPS) else per_device
    return jax.shard_map(
        body,
        mesh=mesh,
        in_specs=(
            P("dp", "slab", None, None, None),
            P("dp", "slab", None, None, None),
            P("slab", "dp", None),
            P(),
            P(),
            P(),
            P(),
        ),
        out_specs=(P("dp", "slab", None, None, None), P("slab", "dp", None)),
        check_vma=False,
    )
```

```python
import functools
import math

import jax
import jax.numpy as jnp
import ml_dtypes
import numpy as np
from jax import lax
from jax.experimental import pallas as pl
from jax.experimental.pallas import tpu as pltpu
from jax.sharding import PartitionSpec as P

C = 64
MX = 16
MY = 16
MZ = 16
NX = 32
NY = 24
NZ = 128


root_half = 0.7071067811865476
inv_root_two_pi = 0.3989422804014327


def dft_table(length, kept_count):
    half_kept = kept_count // 2
    positions = jnp.arange(length, dtype=jnp.int32)
    cos_freq = jnp.arange(half_kept, dtype=jnp.int32)
    freqs = jnp.concatenate([cos_freq, cos_freq + 1])[:, None]
    phases = (freqs * positions[None, :] % length).astype(jnp.float32) * (2.0 * math.pi / length)
    values = jnp.concatenate([jnp.cos(phases[:half_kept]), jnp.sin(phases[half_kept:])], axis=0)
    return values.astype(jnp.bfloat16)


def gelu_value(values_in):
    return 0.5 * values_in * (1.0 + jax.scipy.special.erf(values_in * root_half))


def gelu_slope(values_in):
    return (
        0.5 * (1.0 + jax.scipy.special.erf(values_in * root_half))
        + values_in * jnp.exp(-0.5 * values_in * values_in) * inv_root_two_pi
    )


def bdot(form, left, right):
    return jnp.einsum(form, left, right, preferred_element_type=jnp.float32)


def per_device(inputs, cotangent, spectral_weight, w_in, b_in, w_out, b_out):
    slab_count = lax.axis_size("slab")
    group_count = lax.axis_size("dp")
    local_modes = MY // slab_count
    group_modes = MX * MZ // group_count
    crop_count = inputs.shape[0]
    table_x = dft_table(NX, MX)
    table_y = dft_table(NY, MY)
    table_z = dft_table(NZ, MZ)
    factor = 8.0 / (NX * NY * NZ)

    def analyse(samples):
        along_z = bdot("bxycz,kz->bxyck", samples, table_z).astype(jnp.bfloat16)
        along_y = bdot("bxyck,jy->bxjck", along_z, table_y).astype(jnp.bfloat16)
        return bdot(
            "bxjck,ix->bijck",
            lax.all_to_all(along_y, "slab", split_axis=2, concat_axis=1, tiled=True),
            table_x,
        ).astype(jnp.bfloat16)

    def synthesise(coeff_in):
        back_x = bdot("bijck,ix->bxjck", coeff_in, table_x).astype(jnp.bfloat16)
        back_y = bdot(
            "bxjck,jy->bxyck",
            lax.all_to_all(back_x, "slab", split_axis=1, concat_axis=2, tiled=True),
            table_y,
        ).astype(jnp.bfloat16)
        return bdot("bxyck,kz->bxycz", back_y, table_z) * factor

    def send_out(coeff_in):
        ordered = jnp.transpose(coeff_in, (0, 2, 1, 4, 3)).reshape(
            crop_count, local_modes, group_count, group_modes, C
        )
        arrived = lax.all_to_all(ordered, "dp", split_axis=2, concat_axis=0, tiled=True)
        return arrived.reshape(crop_count * group_count, local_modes, group_modes, C)

    def send_back(mixed_in):
        shaped = mixed_in.reshape(crop_count * group_count, local_modes, 1, group_modes, C)
        arrived = lax.all_to_all(shaped, "dp", split_axis=0, concat_axis=2, tiled=True)
        return jnp.transpose(arrived.reshape(crop_count, local_modes, MX, MZ, C), (0, 2, 1, 4, 3))

    owned = spectral_weight.reshape(local_modes, group_modes, C, C)
    coeffs = analyse(inputs)
    routed = send_out(coeffs)
    mixed_modes = send_back(bdot("bjgc,jgco->bjgo", routed, owned).astype(jnp.bfloat16))
    spectral = synthesise(mixed_modes)
    activation = bdot("bxycz,ch->bxyhz", inputs, w_in) + b_in[:, None]
    hidden = gelu_value(activation).astype(jnp.bfloat16)
    pre_gelu = bdot("bxyhz,hc->bxycz", hidden, w_out) + b_out[:, None] + spectral
    grad_pre = (cotangent.astype(jnp.float32) * gelu_slope(pre_gelu)).astype(jnp.bfloat16)
    grad_act = (bdot("bxycz,hc->bxyhz", grad_pre, w_out) * gelu_slope(activation)).astype(
        jnp.bfloat16
    )
    grad_coeffs = analyse(grad_pre)
    grad_routed = send_out(grad_coeffs)
    back_modes = send_back(bdot("bjgo,jgco->bjgc", grad_routed, owned).astype(jnp.bfloat16))
    grad_weight = (bdot("bjgc,bjgo->jgco", routed, grad_routed) * factor).reshape(
        local_modes, group_modes, C * C
    )
    grad_field = (bdot("bxyhz,ch->bxycz", grad_act, w_in) + synthesise(back_modes)).astype(
        jnp.bfloat16
    )
    return (grad_field, grad_weight)


SLABS = 4
GROUPS = 8
XL = NX // SLABS
JL = MY // SLABS
GM = MX * MZ // GROUPS
HID = 256
UNITS = XL * NY // 4
FACTOR = 8.0 / (NX * NY * NZ)
F32 = jnp.float32
BF16 = jnp.bfloat16
STEP = 512
HALF_LOG2_E = 0.5 / math.log(2.0)


def host_table(length, kept):
    freq = np.concatenate([np.arange(kept // 2), np.arange(kept // 2) + 1])[:, None]
    phase = (freq * np.arange(length)[None, :] % length).astype(np.float32)
    phase = phase * np.float32(2.0 * math.pi / length)
    return np.concatenate([np.cos(phase[: kept // 2]), np.sin(phase[kept // 2 :])], axis=0)


def host_tables():
    eye = np.eye(MZ, dtype=np.float32)
    kz = np.kron(np.eye(8, dtype=np.float32), host_table(NZ, MZ))
    ky = np.kron(host_table(NY, MY), eye)
    kx = np.kron(host_table(NX, MX), eye)
    spread = np.repeat(np.eye(C, dtype=np.float32), C, axis=1)
    tables = (kz, kz.T, ky, ky.T, kx, kx.T, spread, spread.T)
    return tuple(jnp.asarray(np.ascontiguousarray(t).astype(ml_dtypes.bfloat16)) for t in tables)


def dot(left, right):
    return jnp.dot(left, right, preferred_element_type=F32)


def fused_kernel(
    x_hbm, ct_hbm, w_hbm, w_in, b_in, w_out_t, b_out,
    kz, kz_t, ky, ky_t, kx, kx_t, spread, spread_t,
    gx_hbm, gw_hbm,
    x_v, ct_v, w_v, gw_v, slope_v, part_v, gp_v, along_z, rows_v,
    send_s, recv_s, send_g, recv_g, wide_v, first_v, w_out, bias_v,
    send_sem, recv_sem, load_sem, store_sem,
):
    slab = lax.axis_index("slab")
    group = lax.axis_index("dp")

    loads = [
        pltpu.make_async_copy(x_hbm, x_v, load_sem.at[0]),
        pltpu.make_async_copy(ct_hbm, ct_v, load_sem.at[1]),
        pltpu.make_async_copy(w_hbm, w_v, load_sem.at[2]),
    ]
    for load in loads:
        load.start()

    barrier = pltpu.get_barrier_semaphore()
    for r in range(1, SLABS):
        pl.semaphore_signal(
            barrier, inc=1, device_id={"slab": lax.rem(slab + r, SLABS)},
            device_id_type=pl.DeviceIdType.MESH,
        )
    for r in range(1, GROUPS):
        pl.semaphore_signal(
            barrier, inc=1, device_id={"dp": lax.rem(group + r, GROUPS)},
            device_id_type=pl.DeviceIdType.MESH,
        )

    bias = b_in[...]
    high = bias.astype(BF16).astype(F32)
    middle = (bias - high).astype(BF16).astype(F32)
    low = bias - high - middle
    row = lax.broadcasted_iota(jnp.int32, (C, HID), 0)
    bias_rows = jnp.where(row == 0, high, jnp.where(row == 1, middle, jnp.where(row == 2, low, 0.0)))
    first_v[...] = jnp.concatenate([w_in[...].astype(F32), bias_rows], axis=0).T.astype(BF16)
    w_out[...] = w_out_t[...].astype(F32).T.astype(BF16)
    bias_v[...] = jnp.broadcast_to(b_out[...], (128, C)).T

    def exchange(phase, send, recv, axis, me, count):
        copies = []
        for r in range(1, count):
            dest = lax.rem(me + r, count)
            copy = pltpu.make_async_remote_copy(
                src_ref=send.at[dest],
                dst_ref=recv.at[me],
                send_sem=send_sem.at[phase, r - 1],
                recv_sem=recv_sem.at[phase, r - 1],
                device_id={axis: dest},
                device_id_type=pl.DeviceIdType.MESH,
            )
            copy.start()
            copies.append(copy)
        recv[me] = send[me]
        return copies

    def finish(copies):
        for copy in copies:
            copy.wait()

    def over_slabs(phase):
        return exchange(phase, send_s.at[phase // 2], recv_s.at[phase // 2], "slab", slab, SLABS)

    def over_groups(phase):
        return exchange(phase, send_g.at[phase // 2], recv_g.at[phase // 2], "dp", group, GROUPS)

    def lanes_of(ref, plane, first, count):
        return jnp.concatenate([ref[plane * NY + first + q] for q in range(count)], axis=1)

    def send_along_y(phase):
        along_y = dot(along_z[...], ky_t[...])
        for xl in range(XL):
            turned = along_y[xl * C : (xl + 1) * C].T
            for s in range(SLABS):
                for p in range(JL // 2):
                    j = s * JL + 2 * p
                    pair = jnp.concatenate(
                        [turned[j * MZ : (j + 1) * MZ], turned[(j + 1) * MZ : (j + 2) * MZ]], axis=1
                    )
                    send_s[phase // 2, s, xl * MZ : (xl + 1) * MZ, 2 * p * C : 2 * (p + 1) * C] = (
                        pair.astype(BF16)
                    )
        return over_slabs(phase)

    def send_modes(phase):
        arrived = recv_s[(phase - 1) // 2].reshape(NX * MZ, JL * C)
        modes = dot(kx[...], arrived).astype(BF16)
        send_g[phase // 2] = modes.reshape(GROUPS, GM, JL * C)
        return over_groups(phase)

    def send_planes(phase):
        arrived = recv_g[(phase - 1) // 2].reshape(MX * MZ, JL * C)
        planes = dot(kx_t[...], arrived).astype(BF16)
        send_s[phase // 2] = planes.reshape(SLABS, XL * MZ, JL * C)
        return over_slabs(phase)

    def back_along_y(phase):
        for xl in range(XL):
            blocks = []
            for s in range(SLABS):
                rows = recv_s[phase // 2, s, xl * MZ : (xl + 1) * MZ, :].astype(F32)
                for jl in range(JL):
                    blocks.append(rows[:, jl * C : (jl + 1) * C])
            turned = jnp.concatenate(blocks, axis=0).T
            rows_v[xl * C : (xl + 1) * C, :] = turned.astype(BF16)
        along_z[...] = dot(rows_v[...], ky[...]).astype(BF16)

    def plane_rows(xl):
        return pl.ds(pl.multiple_of(xl * C, C), C)

    def forward_units(first, last):
        def unit(u, carry):
            plane, part = u // (NY // 4), lax.rem(u, NY // 4)
            samples = lanes_of(x_v, plane, part * 4, 4)
            ones = jnp.ones((16, 4 * NZ), BF16)
            act = dot(first_v[:, : C + 16], jnp.concatenate([samples, ones], axis=0)).astype(BF16)
            phi = lax.erf(act * root_half) * 0.5 + 0.5
            bell = jnp.exp2(act * act * -HALF_LOG2_E) * inv_root_two_pi
            slope_v[u] = phi + act * bell
            part_v[u] = dot(w_out_t[...], act * phi) + jnp.concatenate([bias_v[...]] * 4, axis=1)
            return carry

        lax.fori_loop(first, last, unit, 0, unroll=2)

    def backward_units(first, last):
        def unit(u, carry):
            grad = dot(w_out[...], gp_v[u]).astype(BF16) * slope_v[u]
            part_v[u] = dot(w_in[...], grad)
            return carry

        lax.fori_loop(first, last, unit, 0, unroll=4)

    loads[0].wait()

    def analyse_plane(xl, carry):
        for t in range(NY // 8):
            samples = lanes_of(x_v, xl, t * 8, 8)
            along_z[plane_rows(xl), t * 128 : (t + 1) * 128] = dot(samples, kz_t[...]).astype(BF16)
        return carry

    lax.fori_loop(0, XL, analyse_plane, 0)
    pl.semaphore_wait(barrier, SLABS + GROUPS - 2)
    flight = send_along_y(0)
    forward_units(0, 12)
    finish(flight)
    flight = send_modes(1)
    forward_units(12, 24)
    finish(flight)

    loads[2].wait()
    coeffs = recv_g.at[0]
    grads = recv_g.at[2]

    def pair_rows(ref, p):
        return ref[:, :, 2 * p * C : 2 * (p + 1) * C].reshape(GROUPS * GM, 2 * C)

    for p in range(JL // 2):
        pair = pair_rows(coeffs, p)
        mixed = []
        for half in range(2):
            jl = 2 * p + half
            rows = pair[:, half * C : (half + 1) * C]

            def mix(n, total, rows=rows, jl=jl):
                span = pl.ds(pl.multiple_of(n * STEP, STEP), STEP)
                wide = dot(rows, spread[:, span])
                wide_v[jl, :, span] = wide.astype(BF16)
                term = (wide.reshape(GROUPS, GM, STEP) * w_v[jl, :, span].astype(F32)[None]).reshape(GROUPS * GM, STEP)
                return total + sum(term[:, q * 128 : (q + 1) * 128] for q in range(STEP // 128))

            total = lax.fori_loop(
                0, C * C // STEP, mix, jnp.zeros((GROUPS * GM, 2 * C), F32), unroll=4
            )
            mixed.append(total[:, :C] + total[:, C:])
        send_g[1, :, :, 2 * p * C : 2 * (p + 1) * C] = (
            jnp.concatenate(mixed, axis=1).astype(BF16).reshape(GROUPS, GM, 2 * C)
        )
    flight = over_groups(2)
    forward_units(24, 36)
    finish(flight)
    flight = send_planes(3)
    forward_units(36, UNITS)
    finish(flight)
    back_along_y(3)

    loads[1].wait()

    def middle_plane(xl, carry):
        for t in range(NY // 8):
            kept = along_z[plane_rows(xl), t * 128 : (t + 1) * 128]
            u = xl * (NY // 4) + 2 * t
            pre = jnp.concatenate([part_v[u], part_v[u + 1]], axis=1) + dot(kept, kz[...]) * FACTOR
            phi = 0.5 + 0.5 * lax.erf(pre * root_half)
            slope = phi + pre * jnp.exp(pre * pre * -0.5) * inv_root_two_pi
            grad = (lanes_of(ct_v, xl, t * 8, 8).astype(F32) * slope).astype(BF16)
            gp_v[u] = grad[:, :512]
            gp_v[u + 1] = grad[:, 512:]
            along_z[plane_rows(xl), t * 128 : (t + 1) * 128] = dot(grad, kz_t[...]).astype(BF16)
        return carry

    lax.fori_loop(0, XL, middle_plane, 0)
    flight = send_along_y(4)
    backward_units(0, 16)
    finish(flight)
    flight = send_modes(5)
    backward_units(16, 32)
    finish(flight)

    for p in range(JL // 2):
        pair = pair_rows(grads, p)
        mixed = []
        for half in range(2):
            jl = 2 * p + half
            rows = pair[:, half * C : (half + 1) * C]
            twice = jnp.concatenate([rows, rows], axis=1)
            wide = jnp.concatenate([twice] * (STEP // 128), axis=1).reshape(GROUPS, GM, STEP)

            def mix_back(n, total, wide=wide, jl=jl):
                span = pl.ds(pl.multiple_of(n * STEP, STEP), STEP)
                term = wide * w_v[jl, :, span][None]
                return total + dot(term.reshape(GROUPS * GM, STEP), spread_t[span, :])

            mixed.append(
                lax.fori_loop(
                    0, C * C // STEP, mix_back, jnp.zeros((GROUPS * GM, C), F32), unroll=4
                )
            )
        send_g[3, :, :, 2 * p * C : 2 * (p + 1) * C] = (
            jnp.concatenate(mixed, axis=1).astype(BF16).reshape(GROUPS, GM, 2 * C)
        )
    flight = over_groups(6)

    for p in range(JL // 2):
        grad_pair = pair_rows(grads, p).astype(F32)
        for half in range(2):
            jl = 2 * p + half
            grad_rows = grad_pair[:, half * C : (half + 1) * C] * FACTOR
            wide = jnp.concatenate([grad_rows, grad_rows], axis=1).reshape(GROUPS, GM, 2 * C)

            def outer(n, carry, wide=wide, jl=jl):
                span = pl.ds(pl.multiple_of(n * 128, 128), 128)
                left = wide_v[jl, :, span].astype(F32).reshape(GROUPS, GM, 2 * C)
                gw_v[jl, :, span] = jnp.sum(left * wide, axis=0)
                return carry

            lax.fori_loop(0, C * C // 128, outer, 0, unroll=4)
    store_gw = pltpu.make_async_copy(gw_v, gw_hbm, store_sem.at[0])
    store_gw.start()
    finish(flight)
    flight = send_planes(7)
    backward_units(32, UNITS)
    finish(flight)
    back_along_y(7)

    def last_plane(xl, carry):
        for t in range(NY // 8):
            kept = along_z[plane_rows(xl), t * 128 : (t + 1) * 128]
            u = xl * (NY // 4) + 2 * t
            total = jnp.concatenate([part_v[u], part_v[u + 1]], axis=1)
            total = (total + dot(kept, kz[...]) * FACTOR).astype(BF16)
            for q in range(8):
                ct_v[xl * NY + t * 8 + q] = total[:, q * NZ : (q + 1) * NZ]
        return carry

    lax.fori_loop(0, XL, last_plane, 0)
    store_gx = pltpu.make_async_copy(ct_v, gx_hbm, store_sem.at[1])
    store_gx.start()
    store_gw.wait()
    store_gx.wait()


def fused_device(inputs, cotangent, spectral_weight, w_in, b_in, w_out, b_out):
    field = inputs.shape
    flat = (XL * NY, C, NZ)
    any_spec = pl.BlockSpec(memory_space=pl.ANY)
    vmem_spec = pl.BlockSpec(memory_space=pltpu.VMEM)
    out = pl.pallas_call(
        fused_kernel,
        out_shape=(
            jax.ShapeDtypeStruct(flat, BF16),
            jax.ShapeDtypeStruct((JL, GM, C * C), F32),
        ),
        in_specs=[any_spec] * 3 + [vmem_spec] * 12,
        out_specs=(any_spec, any_spec),
        scratch_shapes=[
            pltpu.VMEM(flat, BF16),
            pltpu.VMEM(flat, BF16),
            pltpu.VMEM((JL, GM, C * C), BF16),
            pltpu.VMEM((JL, GM, C * C), F32),
            pltpu.VMEM((UNITS, HID, 4 * NZ), BF16),
            pltpu.VMEM((UNITS, C, 4 * NZ), F32),
            pltpu.VMEM((UNITS, C, 4 * NZ), BF16),
            pltpu.VMEM((XL * C, NY * MZ), BF16),
            pltpu.VMEM((XL * C, MY * MZ), BF16),
            pltpu.VMEM((4, SLABS, XL * MZ, JL * C), BF16),
            pltpu.VMEM((4, SLABS, XL * MZ, JL * C), BF16),
            pltpu.VMEM((4, GROUPS, GM, JL * C), BF16),
            pltpu.VMEM((4, GROUPS, GM, JL * C), BF16),
            pltpu.VMEM((JL, GROUPS * GM, C * C), BF16),
            pltpu.VMEM((HID, 2 * C), BF16),
            pltpu.VMEM((HID, C), BF16),
            pltpu.VMEM((C, 128), F32),
            pltpu.SemaphoreType.DMA((8, GROUPS - 1)),
            pltpu.SemaphoreType.DMA((8, GROUPS - 1)),
            pltpu.SemaphoreType.DMA((3,)),
            pltpu.SemaphoreType.DMA((2,)),
        ],
        compiler_params=pltpu.CompilerParams(
            collective_id=0, has_side_effects=True, vmem_limit_bytes=60 * 1024 * 1024
        ),
    )(
        inputs.reshape(flat), cotangent.reshape(flat), spectral_weight,
        w_in, b_in[None], w_out.T, b_out[None], *host_tables(),
    )
    return out[0].reshape(field), out[1]


def solution(mesh):
    sizes = (mesh.shape["slab"], mesh.shape["dp"])
    body = fused_device if sizes == (SLABS, GROUPS) else per_device
    return jax.shard_map(
        body,
        mesh=mesh,
        in_specs=(
            P("dp", "slab", None, None, None),
            P("dp", "slab", None, None, None),
            P("slab", "dp", None),
            P(),
            P(),
            P(),
            P(),
        ),
        out_specs=(P("dp", "slab", None, None, None), P("slab", "dp", None)),
        check_vma=False,
    )
```

```python
import math

import jax
import jax.numpy as jnp
import ml_dtypes
import numpy as np
from jax import lax
from jax.experimental import pallas as pl
from jax.experimental.pallas import tpu as pltpu
from jax.sharding import PartitionSpec as P

C = 64
MX = 16
MY = 16
MZ = 16
NX = 32
NY = 24
NZ = 128


root_half = 0.7071067811865476
inv_root_two_pi = 0.3989422804014327


def dft_table(length, kept_count):
    half_kept = kept_count // 2
    positions = jnp.arange(length, dtype=jnp.int32)
    cos_freq = jnp.arange(half_kept, dtype=jnp.int32)
    freqs = jnp.concatenate([cos_freq, cos_freq + 1])[:, None]
    phases = (freqs * positions[None, :] % length).astype(jnp.float32) * (2.0 * math.pi / length)
    values = jnp.concatenate([jnp.cos(phases[:half_kept]), jnp.sin(phases[half_kept:])], axis=0)
    return values.astype(jnp.bfloat16)


def gelu_value(values_in):
    return 0.5 * values_in * (1.0 + jax.scipy.special.erf(values_in * root_half))


def gelu_slope(values_in):
    return (
        0.5 * (1.0 + jax.scipy.special.erf(values_in * root_half))
        + values_in * jnp.exp(-0.5 * values_in * values_in) * inv_root_two_pi
    )


def bdot(form, left, right):
    return jnp.einsum(form, left, right, preferred_element_type=jnp.float32)


def per_device(inputs, cotangent, spectral_weight, w_in, b_in, w_out, b_out):
    slab_count = lax.axis_size("slab")
    group_count = lax.axis_size("dp")
    local_modes = MY // slab_count
    group_modes = MX * MZ // group_count
    crop_count = inputs.shape[0]
    table_x = dft_table(NX, MX)
    table_y = dft_table(NY, MY)
    table_z = dft_table(NZ, MZ)
    factor = 8.0 / (NX * NY * NZ)

    def analyse(samples):
        along_z = bdot("bxycz,kz->bxyck", samples, table_z).astype(jnp.bfloat16)
        along_y = bdot("bxyck,jy->bxjck", along_z, table_y).astype(jnp.bfloat16)
        return bdot(
            "bxjck,ix->bijck",
            lax.all_to_all(along_y, "slab", split_axis=2, concat_axis=1, tiled=True),
            table_x,
        ).astype(jnp.bfloat16)

    def synthesise(coeff_in):
        back_x = bdot("bijck,ix->bxjck", coeff_in, table_x).astype(jnp.bfloat16)
        back_y = bdot(
            "bxjck,jy->bxyck",
            lax.all_to_all(back_x, "slab", split_axis=1, concat_axis=2, tiled=True),
            table_y,
        ).astype(jnp.bfloat16)
        return bdot("bxyck,kz->bxycz", back_y, table_z) * factor

    def send_out(coeff_in):
        ordered = jnp.transpose(coeff_in, (0, 2, 1, 4, 3)).reshape(
            crop_count, local_modes, group_count, group_modes, C
        )
        arrived = lax.all_to_all(ordered, "dp", split_axis=2, concat_axis=0, tiled=True)
        return arrived.reshape(crop_count * group_count, local_modes, group_modes, C)

    def send_back(mixed_in):
        shaped = mixed_in.reshape(crop_count * group_count, local_modes, 1, group_modes, C)
        arrived = lax.all_to_all(shaped, "dp", split_axis=0, concat_axis=2, tiled=True)
        return jnp.transpose(arrived.reshape(crop_count, local_modes, MX, MZ, C), (0, 2, 1, 4, 3))

    owned = spectral_weight.reshape(local_modes, group_modes, C, C)
    coeffs = analyse(inputs)
    routed = send_out(coeffs)
    mixed_modes = send_back(bdot("bjgc,jgco->bjgo", routed, owned).astype(jnp.bfloat16))
    spectral = synthesise(mixed_modes)
    activation = bdot("bxycz,ch->bxyhz", inputs, w_in) + b_in[:, None]
    hidden = gelu_value(activation).astype(jnp.bfloat16)
    pre_gelu = bdot("bxyhz,hc->bxycz", hidden, w_out) + b_out[:, None] + spectral
    grad_pre = (cotangent.astype(jnp.float32) * gelu_slope(pre_gelu)).astype(jnp.bfloat16)
    grad_act = (bdot("bxycz,hc->bxyhz", grad_pre, w_out) * gelu_slope(activation)).astype(
        jnp.bfloat16
    )
    grad_coeffs = analyse(grad_pre)
    grad_routed = send_out(grad_coeffs)
    back_modes = send_back(bdot("bjgo,jgco->bjgc", grad_routed, owned).astype(jnp.bfloat16))
    grad_weight = (bdot("bjgc,bjgo->jgco", routed, grad_routed) * factor).reshape(
        local_modes, group_modes, C * C
    )
    grad_field = (bdot("bxyhz,ch->bxycz", grad_act, w_in) + synthesise(back_modes)).astype(
        jnp.bfloat16
    )
    return (grad_field, grad_weight)


SLABS = 4
GROUPS = 8
XL = NX // SLABS
JL = MY // SLABS
GM = MX * MZ // GROUPS
HID = 256
UNITS = XL * NY // 4
FACTOR = 8.0 / (NX * NY * NZ)
F32 = jnp.float32
BF16 = jnp.bfloat16
STEP = 512
LAST_STEPS = 4
HALF_LOG2_E = 0.5 / math.log(2.0)


def host_table(length, kept):
    freq = np.concatenate([np.arange(kept // 2), np.arange(kept // 2) + 1])[:, None]
    phase = (freq * np.arange(length)[None, :] % length).astype(np.float32)
    phase = phase * np.float32(2.0 * math.pi / length)
    return np.concatenate([np.cos(phase[: kept // 2]), np.sin(phase[kept // 2 :])], axis=0)


def host_tables():
    eye = np.eye(MZ, dtype=np.float32)
    kz = np.kron(np.eye(8, dtype=np.float32), host_table(NZ, MZ))
    ky = np.kron(host_table(NY, MY), eye)
    kx = np.kron(host_table(NX, MX), eye)
    spread = np.repeat(np.eye(C, dtype=np.float32), C, axis=1)
    tables = (kz, kz.T, ky, ky.T, kx, kx.T, spread, spread.T)
    return tuple(jnp.asarray(np.ascontiguousarray(t).astype(ml_dtypes.bfloat16)) for t in tables)


def dot(left, right):
    return jnp.dot(left, right, preferred_element_type=F32)


def fused_kernel(
    x_hbm, ct_hbm, w_hbm, w_in, b_in, w_out_t, b_out,
    kz, kz_t, ky, ky_t, kx, kx_t, spread, spread_t,
    part_hbm, kept_hbm, gw_hbm,
    x_v, ct_v, w_v, gw_v, slope_v, part_v, gp_v, along_z, rows_v,
    send_s, recv_s, send_g, recv_g, wide_v, first_v, w_out, bias_v,
    send_sem, recv_sem, load_sem, store_sem,
):
    slab = lax.axis_index("slab")
    group = lax.axis_index("dp")

    loads = [
        pltpu.make_async_copy(x_hbm, x_v, load_sem.at[0]),
        pltpu.make_async_copy(ct_hbm, ct_v, load_sem.at[1]),
        pltpu.make_async_copy(w_hbm, w_v, load_sem.at[2]),
    ]
    for load in loads:
        load.start()

    barrier = pltpu.get_barrier_semaphore()
    for r in range(1, SLABS):
        pl.semaphore_signal(
            barrier, inc=1, device_id={"slab": lax.rem(slab + r, SLABS)},
            device_id_type=pl.DeviceIdType.MESH,
        )
    for r in range(1, GROUPS):
        pl.semaphore_signal(
            barrier, inc=1, device_id={"dp": lax.rem(group + r, GROUPS)},
            device_id_type=pl.DeviceIdType.MESH,
        )

    bias = b_in[...]
    high = bias.astype(BF16).astype(F32)
    middle = (bias - high).astype(BF16).astype(F32)
    low = bias - high - middle
    row = lax.broadcasted_iota(jnp.int32, (C, HID), 0)
    bias_rows = jnp.where(row == 0, high, jnp.where(row == 1, middle, jnp.where(row == 2, low, 0.0)))
    first_v[...] = jnp.concatenate([w_in[...].astype(F32), bias_rows], axis=0).T.astype(BF16)
    w_out[...] = w_out_t[...].astype(F32).T.astype(BF16)
    bias_v[...] = jnp.broadcast_to(b_out[...], (128, C)).T

    def exchange(phase, send, recv, axis, me, count):
        copies = []
        for r in range(1, count):
            dest = lax.rem(me + r, count)
            copy = pltpu.make_async_remote_copy(
                src_ref=send.at[dest],
                dst_ref=recv.at[me],
                send_sem=send_sem.at[phase, r - 1],
                recv_sem=recv_sem.at[phase, r - 1],
                device_id={axis: dest},
                device_id_type=pl.DeviceIdType.MESH,
            )
            copy.start()
            copies.append(copy)
        recv[me] = send[me]
        return copies

    def finish(copies):
        for copy in copies:
            copy.wait()

    def over_slabs(phase):
        return exchange(phase, send_s.at[phase // 2], recv_s.at[phase // 2], "slab", slab, SLABS)

    def over_groups(phase):
        return exchange(phase, send_g.at[phase // 2], recv_g.at[phase // 2], "dp", group, GROUPS)

    def lanes_of(ref, plane, first, count):
        return jnp.concatenate([ref[plane * NY + first + q] for q in range(count)], axis=1)

    def send_along_y(phase):
        along_y = dot(along_z[...], ky_t[...])
        for xl in range(XL):
            turned = along_y[xl * C : (xl + 1) * C].T
            for s in range(SLABS):
                for p in range(JL // 2):
                    j = s * JL + 2 * p
                    pair = jnp.concatenate(
                        [turned[j * MZ : (j + 1) * MZ], turned[(j + 1) * MZ : (j + 2) * MZ]], axis=1
                    )
                    send_s[phase // 2, s, xl * MZ : (xl + 1) * MZ, 2 * p * C : 2 * (p + 1) * C] = (
                        pair.astype(BF16)
                    )
        return over_slabs(phase)

    def send_modes(phase):
        arrived = recv_s[(phase - 1) // 2].reshape(NX * MZ, JL * C)
        modes = dot(kx[...], arrived).astype(BF16)
        send_g[phase // 2] = modes.reshape(GROUPS, GM, JL * C)
        return over_groups(phase)

    def send_planes(phase):
        arrived = recv_g[(phase - 1) // 2].reshape(MX * MZ, JL * C)
        planes = dot(kx_t[...], arrived).astype(BF16)
        send_s[phase // 2] = planes.reshape(SLABS, XL * MZ, JL * C)
        return over_slabs(phase)

    def back_along_y(phase):
        for xl in range(XL):
            blocks = []
            for s in range(SLABS):
                rows = recv_s[phase // 2, s, xl * MZ : (xl + 1) * MZ, :].astype(F32)
                for jl in range(JL):
                    blocks.append(rows[:, jl * C : (jl + 1) * C])
            turned = jnp.concatenate(blocks, axis=0).T
            rows_v[xl * C : (xl + 1) * C, :] = turned.astype(BF16)
        along_z[...] = dot(rows_v[...], ky[...]).astype(BF16)

    def plane_rows(xl):
        return pl.ds(pl.multiple_of(xl * C, C), C)

    def forward_units(first, last):
        def unit(u, carry):
            plane, part = u // (NY // 4), lax.rem(u, NY // 4)
            samples = lanes_of(x_v, plane, part * 4, 4)
            ones = jnp.ones((16, 4 * NZ), BF16)
            act = dot(first_v[:, : C + 16], jnp.concatenate([samples, ones], axis=0)).astype(BF16)
            phi = lax.erf(act * root_half) * 0.5 + 0.5
            bell = jnp.exp2(act * act * -HALF_LOG2_E) * inv_root_two_pi
            slope_v[u] = phi + act * bell
            part_v[u] = dot(w_out_t[...], act * phi) + jnp.concatenate([bias_v[...]] * 4, axis=1)
            return carry

        lax.fori_loop(first, last, unit, 0, unroll=4)

    def backward_units(first, last):
        def unit(u, carry):
            grad = dot(w_out[...], gp_v[u]).astype(BF16) * slope_v[u]
            gp_v[u] = dot(w_in[...], grad).astype(BF16)
            return carry

        lax.fori_loop(first, last, unit, 0, unroll=8)

        span = pl.ds(first, last - first)
        store = pltpu.make_async_copy(gp_v.at[span], part_hbm.at[span], store_sem.at[first // 16])
        store.start()
        return store

    loads[0].wait()

    def analyse_plane(xl, carry):
        for t in range(NY // 8):
            samples = lanes_of(x_v, xl, t * 8, 8)
            along_z[plane_rows(xl), t * 128 : (t + 1) * 128] = dot(samples, kz_t[...]).astype(BF16)
        return carry

    lax.fori_loop(0, XL, analyse_plane, 0)
    pl.semaphore_wait(barrier, SLABS + GROUPS - 2)
    flight = send_along_y(0)
    forward_units(0, 12)
    finish(flight)
    flight = send_modes(1)
    forward_units(12, 24)
    finish(flight)

    loads[2].wait()
    coeffs = recv_g.at[0]
    grads = recv_g.at[2]

    def pair_rows(ref, p):
        return ref[:, :, 2 * p * C : 2 * (p + 1) * C].reshape(GROUPS * GM, 2 * C)

    for p in range(JL // 2):
        pair = pair_rows(coeffs, p)
        mixed = []
        for half in range(2):
            jl = 2 * p + half
            rows = pair[:, half * C : (half + 1) * C]

            def mix(n, total, rows=rows, jl=jl):
                span = pl.ds(pl.multiple_of(n * STEP, STEP), STEP)
                wide = dot(rows, spread[:, span])
                wide_v[jl, :, span] = wide.astype(BF16)
                term = (wide.reshape(GROUPS, GM, STEP) * w_v[jl, :, span].astype(F32)[None]).reshape(GROUPS * GM, STEP)
                return total + sum(term[:, q * 128 : (q + 1) * 128] for q in range(STEP // 128))

            total = lax.fori_loop(
                0, C * C // STEP, mix, jnp.zeros((GROUPS * GM, 2 * C), F32), unroll=8
            )
            mixed.append(total[:, :C] + total[:, C:])
        send_g[1, :, :, 2 * p * C : 2 * (p + 1) * C] = (
            jnp.concatenate(mixed, axis=1).astype(BF16).reshape(GROUPS, GM, 2 * C)
        )
    flight = over_groups(2)
    forward_units(24, 36)
    finish(flight)
    flight = send_planes(3)
    forward_units(36, UNITS)
    finish(flight)
    back_along_y(3)

    loads[1].wait()

    def middle_plane(xl, carry):
        for t in range(NY // 8):
            kept = along_z[plane_rows(xl), t * 128 : (t + 1) * 128]
            u = xl * (NY // 4) + 2 * t
            pre = jnp.concatenate([part_v[u], part_v[u + 1]], axis=1) + dot(kept, kz[...]) * FACTOR
            phi = 0.5 + 0.5 * lax.erf(pre * root_half)
            slope = phi + pre * jnp.exp(pre * pre * -0.5) * inv_root_two_pi
            grad = (lanes_of(ct_v, xl, t * 8, 8).astype(F32) * slope).astype(BF16)
            gp_v[u] = grad[:, :512]
            gp_v[u + 1] = grad[:, 512:]
            along_z[plane_rows(xl), t * 128 : (t + 1) * 128] = dot(grad, kz_t[...]).astype(BF16)
        return carry

    lax.fori_loop(0, XL, middle_plane, 0)
    flight = send_along_y(4)
    stores = [backward_units(0, 16)]
    finish(flight)
    flight = send_modes(5)
    stores.append(backward_units(16, 32))
    finish(flight)

    for p in range(JL // 2):
        pair = pair_rows(grads, p)
        mixed = []
        for half in range(2):
            jl = 2 * p + half
            rows = pair[:, half * C : (half + 1) * C]
            twice = jnp.concatenate([rows, rows], axis=1)
            wide = jnp.concatenate([twice] * (STEP // 128), axis=1).reshape(GROUPS, GM, STEP)

            def mix_back(n, total, wide=wide, jl=jl):
                span = pl.ds(pl.multiple_of(n * STEP, STEP), STEP)
                term = wide * w_v[jl, :, span][None]
                return total + dot(term.reshape(GROUPS * GM, STEP), spread_t[span, :])

            mixed.append(
                lax.fori_loop(
                    0, C * C // STEP, mix_back, jnp.zeros((GROUPS * GM, C), F32), unroll=8
                )
            )
        send_g[3, :, :, 2 * p * C : 2 * (p + 1) * C] = (
            jnp.concatenate(mixed, axis=1).astype(BF16).reshape(GROUPS, GM, 2 * C)
        )
    flight = over_groups(6)

    for p in range(JL // 2):
        grad_pair = pair_rows(grads, p).astype(F32)
        for half in range(2):
            jl = 2 * p + half
            grad_rows = grad_pair[:, half * C : (half + 1) * C] * FACTOR
            wide = jnp.concatenate([grad_rows, grad_rows], axis=1).reshape(GROUPS, GM, 2 * C)

            def outer(n, carry, wide=wide, jl=jl):
                span = pl.ds(pl.multiple_of(n * 128, 128), 128)
                left = wide_v[jl, :, span].astype(F32).reshape(GROUPS, GM, 2 * C)
                gw_v[jl, :, span] = jnp.sum(left * wide, axis=0)
                return carry

            lax.fori_loop(0, C * C // 128, outer, 0, unroll=8)
    stores.append(pltpu.make_async_copy(gw_v, gw_hbm, store_sem.at[3]))
    stores[-1].start()
    finish(flight)
    flight = send_planes(7)
    stores.append(backward_units(32, UNITS))
    finish(flight)
    back_along_y(7)

    stores.append(pltpu.make_async_copy(along_z, kept_hbm, store_sem.at[4]))
    stores[-1].start()
    for store in stores:
        store.wait()


def last_kernel(part, kept, weight_grad, kz, field_out, weight_out):
    weight_out[...] = weight_grad[...]
    for xl in range(XL // LAST_STEPS):
        for t in range(NY // 8):
            rows = kept[xl * C : (xl + 1) * C, t * 128 : (t + 1) * 128]
            u = xl * (NY // 4) + 2 * t
            total = jnp.concatenate([part[u], part[u + 1]], axis=1).astype(F32)
            total = (total + dot(rows, kz[...]) * FACTOR).astype(BF16)
            for q in range(8):
                field_out[xl * NY + t * 8 + q] = total[:, q * NZ : (q + 1) * NZ]


def fused_device(inputs, cotangent, spectral_weight, w_in, b_in, w_out, b_out):
    field = inputs.shape
    flat = (XL * NY, C, NZ)
    tables = host_tables()
    any_spec = pl.BlockSpec(memory_space=pl.ANY)
    vmem_spec = pl.BlockSpec(memory_space=pltpu.VMEM)
    part, kept, weight_grad = pl.pallas_call(
        fused_kernel,
        out_shape=(
            jax.ShapeDtypeStruct((UNITS, C, 4 * NZ), BF16),
            jax.ShapeDtypeStruct((XL * C, NY * MZ), BF16),
            jax.ShapeDtypeStruct((JL, GM, C * C), F32),
        ),
        in_specs=[any_spec] * 3 + [vmem_spec] * 12,
        out_specs=(any_spec,) * 3,
        scratch_shapes=[
            pltpu.VMEM(flat, BF16),
            pltpu.VMEM(flat, BF16),
            pltpu.VMEM((JL, GM, C * C), BF16),
            pltpu.VMEM((JL, GM, C * C), F32),
            pltpu.VMEM((UNITS, HID, 4 * NZ), BF16),
            pltpu.VMEM((UNITS, C, 4 * NZ), F32),
            pltpu.VMEM((UNITS, C, 4 * NZ), BF16),
            pltpu.VMEM((XL * C, NY * MZ), BF16),
            pltpu.VMEM((XL * C, MY * MZ), BF16),
            pltpu.VMEM((4, SLABS, XL * MZ, JL * C), BF16),
            pltpu.VMEM((4, SLABS, XL * MZ, JL * C), BF16),
            pltpu.VMEM((4, GROUPS, GM, JL * C), BF16),
            pltpu.VMEM((4, GROUPS, GM, JL * C), BF16),
            pltpu.VMEM((JL, GROUPS * GM, C * C), BF16),
            pltpu.VMEM((HID, 2 * C), BF16),
            pltpu.VMEM((HID, C), BF16),
            pltpu.VMEM((C, 128), F32),
            pltpu.SemaphoreType.DMA((8, GROUPS - 1)),
            pltpu.SemaphoreType.DMA((8, GROUPS - 1)),
            pltpu.SemaphoreType.DMA((3,)),
            pltpu.SemaphoreType.DMA((5,)),
        ],
        compiler_params=pltpu.CompilerParams(
            collective_id=0, has_side_effects=True, vmem_limit_bytes=60 * 1024 * 1024
        ),
    )(
        inputs.reshape(flat), cotangent.reshape(flat), spectral_weight,
        w_in, b_in[None], w_out.T, b_out[None], *tables,
    )
    blocks = (
        pl.BlockSpec((UNITS // LAST_STEPS, C, 4 * NZ), lambda n: (n, 0, 0)),
        pl.BlockSpec((XL * C // LAST_STEPS, NY * MZ), lambda n: (n, 0)),
        pl.BlockSpec((JL // LAST_STEPS, GM, C * C), lambda n: (n, 0, 0)),
        pl.BlockSpec((8 * MZ, 8 * NZ), lambda n: (0, 0)),
        pl.BlockSpec((XL * NY // LAST_STEPS, C, NZ), lambda n: (n, 0, 0)),
        pl.BlockSpec((JL // LAST_STEPS, GM, C * C), lambda n: (n, 0, 0)),
    )
    grad_field, weight_grad = pl.pallas_call(
        last_kernel,
        grid=(LAST_STEPS,),
        out_shape=(
            jax.ShapeDtypeStruct(flat, BF16),
            jax.ShapeDtypeStruct((JL, GM, C * C), F32),
        ),
        in_specs=list(blocks[:4]),
        out_specs=blocks[4:],
        compiler_params=pltpu.CompilerParams(vmem_limit_bytes=60 * 1024 * 1024),
    )(part, kept, weight_grad, tables[0])
    return grad_field.reshape(field), weight_grad


def solution(mesh):
    sizes = (mesh.shape["slab"], mesh.shape["dp"])
    body = fused_device if sizes == (SLABS, GROUPS) else per_device
    return jax.shard_map(
        body,
        mesh=mesh,
        in_specs=(
            P("dp", "slab", None, None, None),
            P("dp", "slab", None, None, None),
            P("slab", "dp", None),
            P(),
            P(),
            P(),
            P(),
        ),
        out_specs=(P("dp", "slab", None, None, None), P("slab", "dp", None)),
        check_vma=False,
    )
```

```python
import math

import jax
import jax.numpy as jnp
import ml_dtypes
import numpy as np
from jax import lax
from jax.experimental import pallas as pl
from jax.experimental.pallas import tpu as pltpu
from jax.sharding import PartitionSpec as P

C = 64
MX = 16
MY = 16
MZ = 16
NX = 32
NY = 24
NZ = 128


root_half = 0.7071067811865476
inv_root_two_pi = 0.3989422804014327


def dft_table(length, kept_count):
    half_kept = kept_count // 2
    positions = jnp.arange(length, dtype=jnp.int32)
    cos_freq = jnp.arange(half_kept, dtype=jnp.int32)
    freqs = jnp.concatenate([cos_freq, cos_freq + 1])[:, None]
    phases = (freqs * positions[None, :] % length).astype(jnp.float32) * (2.0 * math.pi / length)
    values = jnp.concatenate([jnp.cos(phases[:half_kept]), jnp.sin(phases[half_kept:])], axis=0)
    return values.astype(jnp.bfloat16)


def gelu_value(values_in):
    return 0.5 * values_in * (1.0 + jax.scipy.special.erf(values_in * root_half))


def gelu_slope(values_in):
    return (
        0.5 * (1.0 + jax.scipy.special.erf(values_in * root_half))
        + values_in * jnp.exp(-0.5 * values_in * values_in) * inv_root_two_pi
    )


def bdot(form, left, right):
    return jnp.einsum(form, left, right, preferred_element_type=jnp.float32)


def per_device(inputs, cotangent, spectral_weight, w_in, b_in, w_out, b_out):
    slab_count = lax.axis_size("slab")
    group_count = lax.axis_size("dp")
    local_modes = MY // slab_count
    group_modes = MX * MZ // group_count
    crop_count = inputs.shape[0]
    table_x = dft_table(NX, MX)
    table_y = dft_table(NY, MY)
    table_z = dft_table(NZ, MZ)
    factor = 8.0 / (NX * NY * NZ)

    def analyse(samples):
        along_z = bdot("bxycz,kz->bxyck", samples, table_z).astype(jnp.bfloat16)
        along_y = bdot("bxyck,jy->bxjck", along_z, table_y).astype(jnp.bfloat16)
        return bdot(
            "bxjck,ix->bijck",
            lax.all_to_all(along_y, "slab", split_axis=2, concat_axis=1, tiled=True),
            table_x,
        ).astype(jnp.bfloat16)

    def synthesise(coeff_in):
        back_x = bdot("bijck,ix->bxjck", coeff_in, table_x).astype(jnp.bfloat16)
        back_y = bdot(
            "bxjck,jy->bxyck",
            lax.all_to_all(back_x, "slab", split_axis=1, concat_axis=2, tiled=True),
            table_y,
        ).astype(jnp.bfloat16)
        return bdot("bxyck,kz->bxycz", back_y, table_z) * factor

    def send_out(coeff_in):
        ordered = jnp.transpose(coeff_in, (0, 2, 1, 4, 3)).reshape(
            crop_count, local_modes, group_count, group_modes, C
        )
        arrived = lax.all_to_all(ordered, "dp", split_axis=2, concat_axis=0, tiled=True)
        return arrived.reshape(crop_count * group_count, local_modes, group_modes, C)

    def send_back(mixed_in):
        shaped = mixed_in.reshape(crop_count * group_count, local_modes, 1, group_modes, C)
        arrived = lax.all_to_all(shaped, "dp", split_axis=0, concat_axis=2, tiled=True)
        return jnp.transpose(arrived.reshape(crop_count, local_modes, MX, MZ, C), (0, 2, 1, 4, 3))

    owned = spectral_weight.reshape(local_modes, group_modes, C, C)
    coeffs = analyse(inputs)
    routed = send_out(coeffs)
    mixed_modes = send_back(bdot("bjgc,jgco->bjgo", routed, owned).astype(jnp.bfloat16))
    spectral = synthesise(mixed_modes)
    activation = bdot("bxycz,ch->bxyhz", inputs, w_in) + b_in[:, None]
    hidden = gelu_value(activation).astype(jnp.bfloat16)
    pre_gelu = bdot("bxyhz,hc->bxycz", hidden, w_out) + b_out[:, None] + spectral
    grad_pre = (cotangent.astype(jnp.float32) * gelu_slope(pre_gelu)).astype(jnp.bfloat16)
    grad_act = (bdot("bxycz,hc->bxyhz", grad_pre, w_out) * gelu_slope(activation)).astype(
        jnp.bfloat16
    )
    grad_coeffs = analyse(grad_pre)
    grad_routed = send_out(grad_coeffs)
    back_modes = send_back(bdot("bjgo,jgco->bjgc", grad_routed, owned).astype(jnp.bfloat16))
    grad_weight = (bdot("bjgc,bjgo->jgco", routed, grad_routed) * factor).reshape(
        local_modes, group_modes, C * C
    )
    grad_field = (bdot("bxyhz,ch->bxycz", grad_act, w_in) + synthesise(back_modes)).astype(
        jnp.bfloat16
    )
    return (grad_field, grad_weight)


SLABS = 4
GROUPS = 8
XL = NX // SLABS
JL = MY // SLABS
GM = MX * MZ // GROUPS
HID = 256
UNITS = XL * NY // 4
FACTOR = 8.0 / (NX * NY * NZ)
F32 = jnp.float32
BF16 = jnp.bfloat16
STEP = 512
LAST_STEPS = 4
HALF_LOG2_E = 0.5 / math.log(2.0)


def host_table(length, kept):
    freq = np.concatenate([np.arange(kept // 2), np.arange(kept // 2) + 1])[:, None]
    phase = (freq * np.arange(length)[None, :] % length).astype(np.float32)
    phase = phase * np.float32(2.0 * math.pi / length)
    return np.concatenate([np.cos(phase[: kept // 2]), np.sin(phase[kept // 2 :])], axis=0)


def host_tables():
    eye = np.eye(MZ, dtype=np.float32)
    kz = np.kron(np.eye(8, dtype=np.float32), host_table(NZ, MZ))
    ky = np.kron(host_table(NY, MY), eye)
    kx = np.kron(host_table(NX, MX), eye)
    spread = np.repeat(np.eye(C, dtype=np.float32), C, axis=1)
    tables = (kz, kz.T, ky, ky.T, kx, kx.T, spread, spread.T)
    return tuple(jnp.asarray(np.ascontiguousarray(t).astype(ml_dtypes.bfloat16)) for t in tables)


def dot(left, right):
    return jnp.dot(left, right, preferred_element_type=F32)


def fused_kernel(
    x_hbm, ct_hbm, w_hbm, w_in, b_in, w_out_t, b_out,
    kz, kz_t, ky, ky_t, kx, kx_t, spread, spread_t,
    part_hbm, kept_hbm, gw_hbm,
    x_v, ct_v, w_v, gw_v, slope_v, part_v, gp_v, along_z, rows_v,
    send_s, recv_s, send_g, recv_g, wide_v, first_v, w_out, bias_v,
    send_sem, recv_sem, load_sem, store_sem,
):
    slab = lax.axis_index("slab")
    group = lax.axis_index("dp")

    loads = [
        pltpu.make_async_copy(x_hbm, x_v, load_sem.at[0]),
        pltpu.make_async_copy(ct_hbm, ct_v, load_sem.at[1]),
        pltpu.make_async_copy(w_hbm, w_v, load_sem.at[2]),
    ]
    for load in loads:
        load.start()

    barrier = pltpu.get_barrier_semaphore()
    for r in range(1, SLABS):
        pl.semaphore_signal(
            barrier, inc=1, device_id={"slab": lax.rem(slab + r, SLABS)},
            device_id_type=pl.DeviceIdType.MESH,
        )
    for r in range(1, GROUPS):
        pl.semaphore_signal(
            barrier, inc=1, device_id={"dp": lax.rem(group + r, GROUPS)},
            device_id_type=pl.DeviceIdType.MESH,
        )

    bias = b_in[...]
    high = bias.astype(BF16).astype(F32)
    middle = (bias - high).astype(BF16).astype(F32)
    low = bias - high - middle
    row = lax.broadcasted_iota(jnp.int32, (C, HID), 0)
    bias_rows = jnp.where(row == 0, high, jnp.where(row == 1, middle, jnp.where(row == 2, low, 0.0)))
    first_v[...] = jnp.concatenate([w_in[...].astype(F32), bias_rows], axis=0).T.astype(BF16)
    w_out[...] = w_out_t[...].astype(F32).T.astype(BF16)
    bias_v[...] = jnp.broadcast_to(b_out[...], (128, C)).T

    def exchange(phase, send, recv, axis, me, count):
        copies = []
        for r in range(1, count):
            dest = lax.rem(me + r, count)
            copy = pltpu.make_async_remote_copy(
                src_ref=send.at[dest],
                dst_ref=recv.at[me],
                send_sem=send_sem.at[phase, r - 1],
                recv_sem=recv_sem.at[phase, r - 1],
                device_id={axis: dest},
                device_id_type=pl.DeviceIdType.MESH,
            )
            copy.start()
            copies.append(copy)
        recv[me] = send[me]
        return copies

    def finish(copies):
        for copy in copies:
            copy.wait()

    def over_slabs(phase):
        return exchange(phase, send_s.at[phase // 2], recv_s.at[phase // 2], "slab", slab, SLABS)

    def over_groups(phase):
        return exchange(phase, send_g.at[phase // 2], recv_g.at[phase // 2], "dp", group, GROUPS)

    def lanes_of(ref, plane, first, count):
        return jnp.concatenate([ref[plane * NY + first + q] for q in range(count)], axis=1)

    def send_along_y(phase):
        along_y = dot(along_z[...], ky_t[...])
        for xl in range(XL):
            turned = along_y[xl * C : (xl + 1) * C].T
            for s in range(SLABS):
                for p in range(JL // 2):
                    j = s * JL + 2 * p
                    pair = jnp.concatenate(
                        [turned[j * MZ : (j + 1) * MZ], turned[(j + 1) * MZ : (j + 2) * MZ]], axis=1
                    )
                    send_s[phase // 2, s, xl * MZ : (xl + 1) * MZ, 2 * p * C : 2 * (p + 1) * C] = (
                        pair.astype(BF16)
                    )
        return over_slabs(phase)

    def send_modes(phase):
        arrived = recv_s[(phase - 1) // 2].reshape(NX * MZ, JL * C)
        modes = dot(kx[...], arrived).astype(BF16)
        send_g[phase // 2] = modes.reshape(GROUPS, GM, JL * C)
        return over_groups(phase)

    def send_planes(phase):
        arrived = recv_g[(phase - 1) // 2].reshape(MX * MZ, JL * C)
        planes = dot(kx_t[...], arrived).astype(BF16)
        send_s[phase // 2] = planes.reshape(SLABS, XL * MZ, JL * C)
        return over_slabs(phase)

    def back_along_y(phase):
        for xl in range(XL):
            blocks = []
            for s in range(SLABS):
                rows = recv_s[phase // 2, s, xl * MZ : (xl + 1) * MZ, :].astype(F32)
                for jl in range(JL):
                    blocks.append(rows[:, jl * C : (jl + 1) * C])
            turned = jnp.concatenate(blocks, axis=0).T
            rows_v[xl * C : (xl + 1) * C, :] = turned.astype(BF16)
        along_z[...] = dot(rows_v[...], ky[...]).astype(BF16)

    def plane_rows(xl):
        return pl.ds(pl.multiple_of(xl * C, C), C)

    def forward_units(first, last):
        def unit(u, carry):
            plane, part = u // (NY // 4), lax.rem(u, NY // 4)
            samples = lanes_of(x_v, plane, part * 4, 4)
            ones = jnp.ones((16, 4 * NZ), BF16)
            act = dot(first_v[:, : C + 16], jnp.concatenate([samples, ones], axis=0)).astype(BF16)
            phi = lax.erf(act * root_half) * 0.5 + 0.5
            bell = jnp.exp2(act * act * -HALF_LOG2_E) * inv_root_two_pi
            slope_v[u] = phi + act * bell
            part_v[u] = dot(w_out_t[...], act * phi) + jnp.concatenate([bias_v[...]] * 4, axis=1)
            return carry

        lax.fori_loop(first, last, unit, 0, unroll=4)

    def backward_units(first, last):
        def unit(u, carry):
            grad = dot(w_out[...], gp_v[u]).astype(BF16) * slope_v[u]
            gp_v[u] = dot(w_in[...], grad).astype(BF16)
            return carry

        lax.fori_loop(first, last, unit, 0, unroll=8)

        span = pl.ds(first, last - first)
        store = pltpu.make_async_copy(gp_v.at[span], part_hbm.at[span], store_sem.at[first // 16])
        store.start()
        return store

    loads[0].wait()

    def analyse_plane(xl, carry):
        for t in range(NY // 8):
            samples = lanes_of(x_v, xl, t * 8, 8)
            along_z[plane_rows(xl), t * 128 : (t + 1) * 128] = dot(samples, kz_t[...]).astype(BF16)
        return carry

    lax.fori_loop(0, XL, analyse_plane, 0)
    pl.semaphore_wait(barrier, SLABS + GROUPS - 2)
    flight = send_along_y(0)
    forward_units(0, 12)
    finish(flight)
    flight = send_modes(1)
    forward_units(12, 24)
    finish(flight)

    loads[2].wait()
    coeffs = recv_g.at[0]
    grads = recv_g.at[2]

    def pair_rows(ref, p):
        return ref[:, :, 2 * p * C : 2 * (p + 1) * C].reshape(GROUPS * GM, 2 * C)

    for p in range(JL // 2):
        pair = pair_rows(coeffs, p)
        mixed = []
        for half in range(2):
            jl = 2 * p + half
            rows = pair[:, half * C : (half + 1) * C]

            def mix(n, total, rows=rows, jl=jl):
                span = pl.ds(pl.multiple_of(n * STEP, STEP), STEP)
                wide = dot(rows, spread[:, span])
                wide_v[jl, :, span] = wide.astype(BF16)
                term = (wide.reshape(GROUPS, GM, STEP) * w_v[jl, :, span].astype(F32)[None]).reshape(GROUPS * GM, STEP)
                return total + sum(term[:, q * 128 : (q + 1) * 128] for q in range(STEP // 128))

            total = lax.fori_loop(
                0, C * C // STEP, mix, jnp.zeros((GROUPS * GM, 2 * C), F32), unroll=8
            )
            mixed.append(total[:, :C] + total[:, C:])
        send_g[1, :, :, 2 * p * C : 2 * (p + 1) * C] = (
            jnp.concatenate(mixed, axis=1).astype(BF16).reshape(GROUPS, GM, 2 * C)
        )
    flight = over_groups(2)
    forward_units(24, 36)
    finish(flight)
    flight = send_planes(3)
    forward_units(36, UNITS)
    finish(flight)
    back_along_y(3)

    loads[1].wait()

    def middle_plane(xl, carry):
        for t in range(NY // 8):
            kept = along_z[plane_rows(xl), t * 128 : (t + 1) * 128]
            u = xl * (NY // 4) + 2 * t
            pre = jnp.concatenate([part_v[u], part_v[u + 1]], axis=1) + dot(kept, kz[...]) * FACTOR
            pre = pre.astype(BF16)
            phi = 0.5 + 0.5 * lax.erf(pre * root_half)
            slope = phi + pre * (jnp.exp2(pre * pre * -HALF_LOG2_E) * inv_root_two_pi)
            grad = lanes_of(ct_v, xl, t * 8, 8) * slope
            gp_v[u] = grad[:, :512]
            gp_v[u + 1] = grad[:, 512:]
            along_z[plane_rows(xl), t * 128 : (t + 1) * 128] = dot(grad, kz_t[...]).astype(BF16)
        return carry

    lax.fori_loop(0, XL, middle_plane, 0)
    flight = send_along_y(4)
    stores = [backward_units(0, 16)]
    finish(flight)
    flight = send_modes(5)
    stores.append(backward_units(16, 32))
    finish(flight)

    for p in range(JL // 2):
        pair = pair_rows(grads, p)
        mixed = []
        for half in range(2):
            jl = 2 * p + half
            rows = pair[:, half * C : (half + 1) * C]
            twice = jnp.concatenate([rows, rows], axis=1)
            wide = jnp.concatenate([twice] * (STEP // 128), axis=1).reshape(GROUPS, GM, STEP)

            def mix_back(n, total, wide=wide, jl=jl):
                span = pl.ds(pl.multiple_of(n * STEP, STEP), STEP)
                term = wide * w_v[jl, :, span][None]
                return total + dot(term.reshape(GROUPS * GM, STEP), spread_t[span, :])

            mixed.append(
                lax.fori_loop(
                    0, C * C // STEP, mix_back, jnp.zeros((GROUPS * GM, C), F32), unroll=8
                )
            )
        send_g[3, :, :, 2 * p * C : 2 * (p + 1) * C] = (
            jnp.concatenate(mixed, axis=1).astype(BF16).reshape(GROUPS, GM, 2 * C)
        )
    flight = over_groups(6)

    for p in range(JL // 2):
        grad_pair = pair_rows(grads, p).astype(F32)
        for half in range(2):
            jl = 2 * p + half
            grad_rows = grad_pair[:, half * C : (half + 1) * C] * FACTOR
            wide = jnp.concatenate([grad_rows, grad_rows], axis=1).reshape(GROUPS, GM, 2 * C)

            def outer(n, carry, wide=wide, jl=jl):
                span = pl.ds(pl.multiple_of(n * 128, 128), 128)
                left = wide_v[jl, :, span].astype(F32).reshape(GROUPS, GM, 2 * C)
                gw_v[jl, :, span] = jnp.sum(left * wide, axis=0)
                return carry

            lax.fori_loop(0, C * C // 128, outer, 0, unroll=8)
    stores.append(pltpu.make_async_copy(gw_v, gw_hbm, store_sem.at[3]))
    stores[-1].start()
    finish(flight)
    flight = send_planes(7)
    stores.append(backward_units(32, UNITS))
    finish(flight)
    back_along_y(7)

    stores.append(pltpu.make_async_copy(along_z, kept_hbm, store_sem.at[4]))
    stores[-1].start()
    for store in stores:
        store.wait()


def last_kernel(part, kept, weight_grad, kz, field_out, weight_out):
    weight_out[...] = weight_grad[...]
    for xl in range(XL // LAST_STEPS):
        for t in range(NY // 8):
            rows = kept[xl * C : (xl + 1) * C, t * 128 : (t + 1) * 128]
            u = xl * (NY // 4) + 2 * t
            total = jnp.concatenate([part[u], part[u + 1]], axis=1).astype(F32)
            total = (total + dot(rows, kz[...]) * FACTOR).astype(BF16)
            for q in range(8):
                field_out[xl * NY + t * 8 + q] = total[:, q * NZ : (q + 1) * NZ]


def fused_device(inputs, cotangent, spectral_weight, w_in, b_in, w_out, b_out):
    field = inputs.shape
    flat = (XL * NY, C, NZ)
    tables = host_tables()
    any_spec = pl.BlockSpec(memory_space=pl.ANY)
    vmem_spec = pl.BlockSpec(memory_space=pltpu.VMEM)
    part, kept, weight_grad = pl.pallas_call(
        fused_kernel,
        out_shape=(
            jax.ShapeDtypeStruct((UNITS, C, 4 * NZ), BF16),
            jax.ShapeDtypeStruct((XL * C, NY * MZ), BF16),
            jax.ShapeDtypeStruct((JL, GM, C * C), F32),
        ),
        in_specs=[any_spec] * 3 + [vmem_spec] * 12,
        out_specs=(any_spec,) * 3,
        scratch_shapes=[
            pltpu.VMEM(flat, BF16),
            pltpu.VMEM(flat, BF16),
            pltpu.VMEM((JL, GM, C * C), BF16),
            pltpu.VMEM((JL, GM, C * C), F32),
            pltpu.VMEM((UNITS, HID, 4 * NZ), BF16),
            pltpu.VMEM((UNITS, C, 4 * NZ), F32),
            pltpu.VMEM((UNITS, C, 4 * NZ), BF16),
            pltpu.VMEM((XL * C, NY * MZ), BF16),
            pltpu.VMEM((XL * C, MY * MZ), BF16),
            pltpu.VMEM((4, SLABS, XL * MZ, JL * C), BF16),
            pltpu.VMEM((4, SLABS, XL * MZ, JL * C), BF16),
            pltpu.VMEM((4, GROUPS, GM, JL * C), BF16),
            pltpu.VMEM((4, GROUPS, GM, JL * C), BF16),
            pltpu.VMEM((JL, GROUPS * GM, C * C), BF16),
            pltpu.VMEM((HID, 2 * C), BF16),
            pltpu.VMEM((HID, C), BF16),
            pltpu.VMEM((C, 128), F32),
            pltpu.SemaphoreType.DMA((8, GROUPS - 1)),
            pltpu.SemaphoreType.DMA((8, GROUPS - 1)),
            pltpu.SemaphoreType.DMA((3,)),
            pltpu.SemaphoreType.DMA((5,)),
        ],
        compiler_params=pltpu.CompilerParams(
            collective_id=0, has_side_effects=True, vmem_limit_bytes=60 * 1024 * 1024
        ),
    )(
        inputs.reshape(flat), cotangent.reshape(flat), spectral_weight,
        w_in, b_in[None], w_out.T, b_out[None], *tables,
    )
    blocks = (
        pl.BlockSpec((UNITS // LAST_STEPS, C, 4 * NZ), lambda n: (n, 0, 0)),
        pl.BlockSpec((XL * C // LAST_STEPS, NY * MZ), lambda n: (n, 0)),
        pl.BlockSpec((JL // LAST_STEPS, GM, C * C), lambda n: (n, 0, 0)),
        pl.BlockSpec((8 * MZ, 8 * NZ), lambda n: (0, 0)),
        pl.BlockSpec((XL * NY // LAST_STEPS, C, NZ), lambda n: (n, 0, 0)),
        pl.BlockSpec((JL // LAST_STEPS, GM, C * C), lambda n: (n, 0, 0)),
    )
    grad_field, weight_grad = pl.pallas_call(
        last_kernel,
        grid=(LAST_STEPS,),
        out_shape=(
            jax.ShapeDtypeStruct(flat, BF16),
            jax.ShapeDtypeStruct((JL, GM, C * C), F32),
        ),
        in_specs=list(blocks[:4]),
        out_specs=blocks[4:],
        compiler_params=pltpu.CompilerParams(vmem_limit_bytes=60 * 1024 * 1024),
    )(part, kept, weight_grad, tables[0])
    return grad_field.reshape(field), weight_grad


def solution(mesh):
    sizes = (mesh.shape["slab"], mesh.shape["dp"])
    body = fused_device if sizes == (SLABS, GROUPS) else per_device
    return jax.shard_map(
        body,
        mesh=mesh,
        in_specs=(
            P("dp", "slab", None, None, None),
            P("dp", "slab", None, None, None),
            P("slab", "dp", None),
            P(),
            P(),
            P(),
            P(),
        ),
        out_specs=(P("dp", "slab", None, None, None), P("slab", "dp", None)),
        check_vma=False,
    )
```
